256 devices in a mesh: dp: 16 (over z_lo, x, core), layer: 16 (over z_hi, y).
Axes of the slice: x: 4, y: 4, z: 8 (z_hi: 4, z_lo: 2; z = z_hi * 2 + z_lo), core: 2. Of those that a mesh axis runs over, the one named last changes fastest.
Arguments:
- query_grads: bfloat16 [256, 2, 16, 4096], P(('dp', 'layer')), may hold values from -6 to 6
- corpus_grads: bfloat16 [24576, 16, 4096], P('dp', 'layer'), may hold values from -240 to 240
- left_inverse: float32 [16, 64, 64], P('layer'), may hold values from -2.5 to 2.5
- right_inverse: float32 [16, 64, 64], P('layer'), may hold values from -2.5 to 2.5
Outputs:
- scores: float32 [256, 2, 24576], P('layer', None, 'dp')
The draws below stay inside these ranges and needn't reach their ends.
All inputs are finite; a program needn't handle non-finite values.
Results may differ from the reference program's by a relative error of at most 0.0029.
Values may be sent and summed in bfloat16 or wider, within the bound.
No kernel may reach another device: no remote copies, remote signals or barrier semaphores. Data moves between devices by JAX's collectives and lax.ppermute only.
A program may use at most 128 MiB of HBM per device.

```python
import jax
import jax.numpy as jnp
from jax import lax

D_IN = 64
D_OUT = 64
K = 4096
BATCHES = 2
QB = 256
LAYERS = 16
N_CORPUS = 24576


def draw_corpus_grads(key, part):
    key = jax.random.fold_in(key, 11)
    key_main, key_rows = jax.random.split(key, 2)
    layer_scale = 1.0 + 2.0 * jnp.arange(LAYERS, dtype=jnp.float32) / (LAYERS - 1)
    rows = jnp.exp(jax.random.uniform(key_rows, (N_CORPUS, 1, 1), jnp.float32, 0.0, jnp.log(10.0)))
    base = jnp.clip(jax.random.normal(key_main, (N_CORPUS, LAYERS, K), jnp.float32), -4.0, 4.0)
    values = base * rows * layer_scale[None, :, None]
    return values.astype(jnp.bfloat16)


def factor_draw(key, count, order):
    key_scale, key_off = jax.random.split(key)
    scale = jnp.exp(jax.random.uniform(key_scale, (count, 1, 1), jnp.float32, jnp.log(0.5), jnp.log(2.0)))
    noise = jnp.clip(jax.random.normal(key_off, (count, order, order), jnp.float32), -4.0, 4.0)
    eye = jnp.eye(order, dtype=jnp.float32)[None, :, :]
    return jnp.clip(scale * (eye + 0.4 * noise / jnp.sqrt(order * 1.0)), -2.5, 2.5)


def draw_left_inverse(key, part):
    key = jax.random.fold_in(key, 23)
    return factor_draw(key, LAYERS, D_IN)


def draw_right_inverse(key, part):
    key = jax.random.fold_in(key, 37)
    return factor_draw(key, LAYERS, D_OUT)


def block_scale(own_key, shape, cuts, least, largest):
    level, own = 1.0, jax.random.fold_in(own_key, 6)
    for axis_at, shards_of in cuts:
        draws = jnp.exp(jax.random.uniform(jax.random.fold_in(own, axis_at), (shards_of,), jnp.float32, least / len(cuts), largest / len(cuts)))
        level = level * jnp.repeat(draws, shape[axis_at] // shards_of).reshape([-1 if axis == axis_at else 1 for axis in range(len(shape))])
    return level


def gaussian(rng, extent, scale, limit, cuts=(), held_as=jnp.bfloat16):
    loudness = block_scale(rng, extent, cuts, -0.22, 0.18) if cuts else 1.0
    array = jax.random.normal(rng, extent, jnp.float32) * scale * loudness
    return jnp.minimum(jnp.maximum(array, -limit), limit).astype(held_as)


def setup_inputs(seed: int = 0) -> dict:
    keys = jax.random.split(jax.random.key(seed), 5)
    return {
        "query_grads": gaussian(keys[0], (QB, BATCHES, LAYERS, K), 1.0, 6.0, ((0, 256),)),
        "corpus_grads": draw_corpus_grads(jax.random.fold_in(keys[4], 71), 0),
        "left_inverse": draw_left_inverse(jax.random.fold_in(keys[4], 71), 0),
        "right_inverse": draw_right_inverse(jax.random.fold_in(keys[4], 71), 0),
    }


def precondition(raw, left, right):
    rows, groups, count, width = raw.shape
    din = left.shape[1]
    dout = right.shape[1]
    values = raw.astype(jnp.float32).reshape(rows, groups, count, din, dout)
    result = jnp.einsum('lai,rblij,ljc->rblac', left, values, right, precision=lax.Precision.HIGHEST)
    return result.reshape(rows, groups, count, din * dout).astype(jnp.bfloat16)

def reference(query_grads, corpus_grads, left_inverse, right_inverse):
    ready = precondition(query_grads, left_inverse, right_inverse)
    ready_layers = jnp.moveaxis(ready, 2, 0)
    corpus_layers = jnp.moveaxis(corpus_grads, 1, 0)

    def step(carry, pieces):
        totals, power = carry
        query_layer, corpus_layer = pieces
        flat = query_layer.reshape(QB * BATCHES, K)
        part = lax.dot_general(flat, corpus_layer, (((1,), (1,)), ((), ())), preferred_element_type=jnp.float32)
        wide = corpus_layer.astype(jnp.float32)
        return ((totals + part.reshape(QB, BATCHES, N_CORPUS), power + lax.optimization_barrier(jnp.sum(wide * wide, axis=1))), None)
    start = (jnp.zeros((QB, BATCHES, N_CORPUS), jnp.float32), jnp.zeros((N_CORPUS,), jnp.float32))
    (totals, power), _ = lax.scan(step, start, (ready_layers, corpus_layers))
    factor = lax.rsqrt(power / (LAYERS * K) + 1e-06)
    return totals * factor[None, None, :]
```

```python
import functools

import jax
import jax.numpy as jnp
from jax import lax
from jax.experimental import pallas as pl
from jax.experimental.pallas import tpu as pltpu
from jax.sharding import PartitionSpec as P

F32, BF16 = jnp.float32, jnp.bfloat16
SIZES = {"zl": 2, "x": 4, "c": 2, "zh": 4, "y": 4}
ROWS, WIDTH, LAYERS = 32, 4096, 16
VMEM_LIMIT = 56 * 1024 * 1024


def whole(*shape):
    return pl.BlockSpec(shape, lambda *_: (0,) * len(shape))


def any_space():
    return pl.BlockSpec(memory_space=pl.ANY)


def shifted(value, **shift):
    pairs = []
    for index in range(256):
        dp, layer = divmod(index, 16)
        at = {"zl": dp // 8, "x": dp // 2 % 4, "c": dp % 2, "zh": layer // 4, "y": layer % 4}
        for name, by in shift.items():
            at[name] = (at[name] + by) % SIZES[name]
        pairs.append((index, (at["zl"] * 8 + at["x"] * 2 + at["c"]) * 16 + at["zh"] * 4 + at["y"]))
    return lax.ppermute(value, ("dp", "layer"), pairs)


def pack_kernel(x_ref, out_ref, scratch):
    for b in range(2):
        for r in range(32):
            piece = x_ref[b, :, r * 128 : (r + 1) * 128].astype(F32)
            scratch[pl.ds(b * 32 + r, LAYERS, stride=64), :] = piece
    out_ref[...] = scratch[...].astype(BF16).reshape(LAYERS, 64, 128)


def pack(x):
    return pl.pallas_call(
        pack_kernel,
        out_shape=jax.ShapeDtypeStruct((LAYERS, 64, 128), BF16),
        scratch_shapes=[pltpu.VMEM((LAYERS * 64, 128), F32)],
        compiler_params=pltpu.CompilerParams(vmem_limit_bytes=VMEM_LIMIT),
        cost_estimate=pl.CostEstimate(flops=0, bytes_accessed=524288, transcendentals=0),
        name="pack",
    )(x)


def ready_kernel(x_ref, left_ref, right_ref, out_ref, scratch):
    right = right_ref[...]
    x = x_ref[...].reshape(16 * 64, 128).astype(F32)
    y = jnp.dot(x, right, precision=lax.Precision.HIGHEST, preferred_element_type=F32)
    wide = jnp.concatenate([y[i * 32 : (i + 1) * 32] for i in range(32)], axis=1)
    z = jnp.dot(left_ref[...], wide, precision=lax.Precision.HIGHEST, preferred_element_type=F32)
    low = lax.broadcasted_iota(jnp.int32, (32, 128), 1) < 64
    for i in range(32):
        part = z[:, i * 128 : (i + 1) * 128]
        even, odd = part[0:32], part[32:64]
        even2, odd2 = part[64:96], part[96:128]
        first = even + pltpu.roll(odd, 64, 1)
        second = pltpu.roll(even2, 64, 1) + odd2
        scratch[i * 32 : (i + 1) * 32, :] = jnp.where(low, first, second)
    for r in range(32):
        out_ref[:, r * 128 : (r + 1) * 128] = scratch[pl.ds(r, 32, stride=32), :].astype(BF16)


def make_ready(x, left, right):
    zero = jnp.zeros_like(right)
    diagonal = jnp.concatenate(
        [jnp.concatenate([right, zero], 1), jnp.concatenate([zero, right], 1)], 0
    )
    spread = left.reshape(32, 2, 32, 2).transpose(1, 3, 0, 2).reshape(128, 32)
    return pl.pallas_call(
        ready_kernel,
        out_shape=jax.ShapeDtypeStruct((ROWS, WIDTH), BF16),
        scratch_shapes=[pltpu.VMEM((1024, 128), F32)],
        compiler_params=pltpu.CompilerParams(vmem_limit_bytes=VMEM_LIMIT),
        cost_estimate=pl.CostEstimate(flops=2**28, bytes_accessed=2**19, transcendentals=0),
        name="ready",
    )(x, spread, diagonal)


def power_kernel(corpus_ref, out_ref):
    block = corpus_ref[...].astype(F32)
    total = block[:, :128] * block[:, :128]
    for r in range(1, 32):
        piece = block[:, r * 128 : (r + 1) * 128]
        total = total + piece * piece
    out_ref[...] = lax.dot_general(
        jnp.ones((8, 128), F32),
        total,
        (((1,), (1,)), ((), ())),
        precision=lax.Precision.HIGHEST,
        preferred_element_type=F32,
    )


def make_power(corpus):
    examples = corpus.shape[0]
    step = 256
    return pl.pallas_call(
        power_kernel,
        grid=(examples // step,),
        in_specs=[pl.BlockSpec((step, WIDTH), lambda i: (i, 0))],
        out_specs=pl.BlockSpec((8, step), lambda i: (0, i)),
        out_shape=jax.ShapeDtypeStruct((8, examples), F32),
        compiler_params=pltpu.CompilerParams(vmem_limit_bytes=VMEM_LIMIT),
        cost_estimate=pl.CostEstimate(flops=2**24, bytes_accessed=12 * 2**20, transcendentals=0),
        name="power",
    )(corpus)


def position(chunk):
    a, k, e = chunk
    dp, layer = lax.axis_index("dp"), lax.axis_index("layer")
    zl, x, c = (dp // 8 + a) % 2, (dp // 2 + 4 - k) % 4, (dp + e) % 2
    zh, y = zl * 2 + x // 2, (x % 2) * 2 + c
    return ((y + 4 - layer % 4) % 4) * 4 + zh


def dot_kernel(chunks, *refs):
    count = len(chunks)
    pieces, corpus_ref = refs[:count], refs[count]
    outs = refs[count + 1 : count + 5]
    rows, sems = refs[count + 5 :]

    @pl.when(pl.program_id(0) == 0)
    def _():
        copies = []
        for n, chunk in enumerate(chunks):
            start = pl.multiple_of(position(chunk) * ROWS, ROWS)
            copies.append(
                pltpu.make_async_copy(pieces[n], rows.at[pl.ds(start, ROWS)], sems.at[n])
            )
        for copy in copies:
            copy.start()
        for copy in copies:
            copy.wait()

    total = lax.dot_general(
        rows[...], corpus_ref[...], (((1,), (1,)), ((), ())), preferred_element_type=F32
    )
    for k in range(4):
        part = total[k * 128 : (k + 1) * 128].astype(BF16)
        outs[k][...] = part.reshape(4, ROWS, part.shape[1])


def make_totals(chunks, pieces, corpus):
    examples = corpus.shape[0]
    step = 256
    return pl.pallas_call(
        functools.partial(dot_kernel, chunks),
        grid=(examples // step,),
        in_specs=[any_space()] * len(chunks) + [pl.BlockSpec((step, WIDTH), lambda i: (i, 0))],
        out_specs=[pl.BlockSpec((4, ROWS, step), lambda i: (0, 0, i))] * 4,
        out_shape=[jax.ShapeDtypeStruct((4, ROWS, examples), BF16)] * 4,
        scratch_shapes=[
            pltpu.VMEM((512, WIDTH), BF16),
            pltpu.SemaphoreType.DMA((len(chunks),)),
        ],
        compiler_params=pltpu.CompilerParams(vmem_limit_bytes=VMEM_LIMIT),
        cost_estimate=pl.CostEstimate(
            flops=2 * 512 * examples * WIDTH, bytes_accessed=18 * 2**20, transcendentals=0
        ),
        name="totals",
    )(*pieces, corpus)


def add_kernel(*refs):
    ins, outs = refs[:4], refs[4:]
    zh = lax.axis_index("layer") // 4
    for m in range(4):
        at = (zh + m) % 4
        total = ins[0][at].astype(F32)
        for k in range(1, 4):
            total = total + ins[k][at].astype(F32)
        outs[m][...] = total.astype(outs[m].dtype)


def add_y(parts):
    examples = parts[0].shape[2]
    return pl.pallas_call(
        add_kernel,
        out_shape=[
            jax.ShapeDtypeStruct((ROWS, examples), F32 if m == 0 else BF16) for m in range(4)
        ],
        compiler_params=pltpu.CompilerParams(vmem_limit_bytes=VMEM_LIMIT),
        cost_estimate=pl.CostEstimate(flops=2**20, bytes_accessed=2 * 2**20, transcendentals=0),
        name="add_y",
    )(*parts)


def final_kernel(entries, own, a, b, c, p0, p1, p2, p3, out_ref):
    power = p0[0:1] + p1[0:1] + p2[0:1] + p3[0:1]
    factor = lax.rsqrt(power / entries + 1e-06)
    total = own[...] + a[...].astype(F32) + b[...].astype(F32) + c[...].astype(F32)
    out_ref[...] = (total * factor).reshape(out_ref.shape)


def finish(parts, powers, entries):
    examples = parts[0].shape[1]
    return pl.pallas_call(
        functools.partial(final_kernel, entries),
        out_shape=jax.ShapeDtypeStruct((16, 2, examples), F32),
        compiler_params=pltpu.CompilerParams(vmem_limit_bytes=VMEM_LIMIT),
        cost_estimate=pl.CostEstimate(flops=2**20, bytes_accessed=2**20, transcendentals=0),
        name="finish",
    )(*parts, *powers)


def per_device(query_grads, corpus_grads, left_inverse, right_inverse):
    corpus = corpus_grads.reshape(corpus_grads.shape[0], WIDTH)
    power = make_power(corpus)
    owned = lax.all_to_all(pack(query_grads[0]), "layer", 0, 0, tiled=True)
    own = make_ready(owned, left_inverse[0], right_inverse[0])

    pieces = {(0, 0): own}
    for k in (1, 3, 2):
        pieces[0, k] = shifted(own, x=k)
    pieces[1, 0] = shifted(own, zl=1)
    for k in (1, 3, 2):
        pieces[1, k] = shifted(pieces[1, 0], x=k)
    both = {}
    for (a, k), piece in pieces.items():
        both[a, k, 0] = piece
        both[a, k, 1] = shifted(piece, c=1)

    power = power + sum(shifted(power, y=k) for k in (1, 2, 3))
    powers = [power] + [shifted(power, zh=k) for k in (1, 2, 3)]

    chunks = list(both)
    totals = make_totals(chunks, [both[chunk] for chunk in chunks], corpus)
    parts = add_y([totals[0]] + [shifted(totals[k], y=k) for k in (1, 3, 2)])
    sums = [parts[0]] + [shifted(parts[m], zh=m) for m in (1, 3, 2)]
    return finish(sums, powers, WIDTH * LAYERS)


def solution(mesh):
    return jax.shard_map(
        per_device,
        mesh=mesh,
        in_specs=(
            P(("dp", "layer"), None, None, None),
            P("dp", "layer", None),
            P("layer", None, None),
            P("layer", None, None),
        ),
        out_specs=P("layer", None, "dp"),
        check_vma=False,
    )
```

```python
import functools

import jax
import jax.numpy as jnp
from jax import lax
from jax.experimental import pallas as pl
from jax.experimental.pallas import tpu as pltpu
from jax.sharding import PartitionSpec as P

F32, BF16 = jnp.float32, jnp.bfloat16
SIZES = {"zl": 2, "x": 4, "c": 2, "zh": 4, "y": 4}
ROWS, WIDTH, LAYERS = 32, 4096, 16
MIB = 1024 * 1024
FETCHES, AHEAD, PARTS = 3, 2, 16
VMEM = pl.BlockSpec(memory_space=pltpu.VMEM)


def kernel_call(body, name, out_shape, args, flops, moved, limit=4, **more):
    single = not isinstance(out_shape, list)
    return pl.pallas_call(
        body,
        in_specs=[VMEM] * len(args),
        out_specs=VMEM if single else [VMEM] * len(out_shape),
        out_shape=out_shape,
        compiler_params=pltpu.CompilerParams(vmem_limit_bytes=limit * MIB),
        cost_estimate=pl.CostEstimate(flops=flops, bytes_accessed=moved, transcendentals=0),
        name=name,
        **more,
    )(*args)


def shape(*sizes, dtype=BF16):
    return jax.ShapeDtypeStruct(sizes, dtype)


def shifted(value, keep=None, **shift):
    pairs = []
    for index in range(256):
        dp, layer = divmod(index, 16)
        at = {"zl": dp // 8, "x": dp // 2 % 4, "c": dp % 2, "zh": layer // 4, "y": layer % 4}
        for name, by in shift.items():
            at[name] = (at[name] + by) % SIZES[name]
        if keep is None or keep(at):
            to = (at["zl"] * 8 + at["x"] * 2 + at["c"]) * 16 + at["zh"] * 4 + at["y"]
            pairs.append((index, to))
    return lax.ppermute(value, ("dp", "layer"), pairs)


def pack_kernel(x_ref, out_ref, scratch):
    for b in range(2):
        for r in range(32):
            piece = x_ref[b, :, r * 128 : (r + 1) * 128].astype(F32)
            scratch[pl.ds(b * 32 + r, LAYERS, stride=64), :] = piece
    out_ref[...] = scratch[...].astype(BF16).reshape(LAYERS, 64, 128)


def pack(x):
    return kernel_call(
        pack_kernel,
        "pack",
        shape(LAYERS, 64, 128),
        [x],
        0,
        2**19,
        scratch_shapes=[pltpu.VMEM((LAYERS * 64, 128), F32)],
    )


def split(value, count):
    pieces = []
    for _ in range(count):
        piece = value.astype(BF16)
        value = value - piece.astype(F32)
        pieces.append(piece)
    return pieces


def product(a, b):
    return jnp.dot(a, b, preferred_element_type=F32)


def factors_kernel(left_ref, right_ref, left_out, right_out):
    row = lax.broadcasted_iota(jnp.int32, (64, 128), 0)
    lane = lax.broadcasted_iota(jnp.int32, (64, 128), 1) % 64
    twice = jnp.where(row == lane, 1.0, 0.0).astype(BF16)
    spread = jnp.where(row == 2 * (lane % 32) + lane // 32, 1.0, 0.0).astype(BF16)
    row = lax.broadcasted_iota(jnp.int32, (64, 64), 0)
    lane = lax.broadcasted_iota(jnp.int32, (64, 64), 1)
    gather = jnp.where(lane == 2 * (row % 32) + row // 32, 1.0, 0.0).astype(BF16)
    zero = jnp.zeros((64, 128), BF16)
    for n, piece in enumerate(split(right_ref[...], 3)):
        double = product(piece, twice).astype(BF16)
        right_out[0:64, n * 256 : n * 256 + 128] = double
        right_out[0:64, n * 256 + 128 : n * 256 + 256] = zero
        right_out[64:128, n * 256 : n * 256 + 128] = zero
        right_out[64:128, n * 256 + 128 : n * 256 + 256] = double
    for n, piece in enumerate(split(left_ref[...], 2)):
        rows = product(gather, piece).astype(BF16)
        left_out[:, n * 128 : (n + 1) * 128] = product(rows, spread).astype(BF16)


def make_factors(left, right):
    return kernel_call(
        factors_kernel,
        "factors",
        [shape(64, 256), shape(128, 768)],
        [left, right],
        2**22,
        2**18,
    )


def ready_kernel(x_ref, left_ref, right_ref, out_ref, scratch):
    x = x_ref[...].reshape(16 * 64, 128)
    y = product(x, right_ref[:, 0:256])
    y = y + product(x, right_ref[:, 256:512])
    y = y + product(x, right_ref[:, 512:768])
    high = y.astype(BF16)
    low = (y - high.astype(F32)).astype(BF16)
    stacks = []
    for i in range(32):
        at = slice(i * 32, (i + 1) * 32)
        column = jnp.concatenate(
            [high[at, :128], high[at, 128:], low[at, :128], low[at, 128:]], axis=0
        )
        stacks.append(jnp.concatenate([column, column], axis=0))
    z = product(left_ref[...], jnp.concatenate(stacks, axis=1))
    first = lax.broadcasted_iota(jnp.int32, (32, 128), 1) < 64
    for i in range(32):
        part = z[:, i * 128 : (i + 1) * 128]
        scratch[i * 32 : (i + 1) * 32, :] = jnp.where(first, part[0:32], part[32:64])
    for r in range(32):
        out_ref[:, r * 128 : (r + 1) * 128] = scratch[pl.ds(r, 32, stride=32), :].astype(BF16)


def make_ready(x, left, right):
    return kernel_call(
        ready_kernel,
        "ready",
        shape(ROWS, WIDTH),
        [x, left, right],
        2**28,
        2**19,
        scratch_shapes=[pltpu.VMEM((1024, 128), F32)],
    )


def fetch(corpus_ref, held_ref, sems, use):
    count = sems.shape[0]
    step = corpus_ref.shape[0] // count

    def copy(start, size, n):
        at = pl.ds(start, size)
        return pltpu.make_async_copy(corpus_ref.at[at], held_ref.at[at], sems.at[n])

    def begin(n):
        for part in range(PARTS):
            copy(n * step + part * step // PARTS, step // PARTS, n).start()

    for n in range(AHEAD):
        begin(n)
    for n in range(count):
        copy(n * step, step, n).wait()
        if n + AHEAD < count:
            begin(n + AHEAD)
        use(n * step, step)


def power_kernel(corpus_ref, out_ref, held_ref, sems):
    def use(start, step):
        totals = []
        for s in range(start, start + step, 32):
            total = None
            for r in range(32):
                piece = held_ref[s : s + 32, r * 128 : (r + 1) * 128].astype(F32)
                total = piece * piece if total is None else total + piece * piece
            totals.append(total)
        power = lax.dot_general(
            jnp.ones((8, 128), F32),
            jnp.concatenate(totals, axis=0),
            (((1,), (1,)), ((), ())),
            precision=lax.Precision.HIGHEST,
            preferred_element_type=F32,
        )[0:1]
        for j in range(step // 128):
            row = start // 128 + j
            out_ref[row : row + 1, :] = power[:, j * 128 : (j + 1) * 128]

    fetch(corpus_ref, held_ref, sems, use)


def corpus_call(body, name, out_shape, args, flops, scratch, limit=50):
    single = not isinstance(out_shape, list)
    return pl.pallas_call(
        body,
        in_specs=[VMEM] * (len(args) - 1) + [pl.BlockSpec(memory_space=pl.ANY)],
        out_specs=VMEM if single else [VMEM] * len(out_shape),
        out_shape=out_shape,
        scratch_shapes=[*scratch, pltpu.SemaphoreType.DMA((FETCHES,))],
        compiler_params=pltpu.CompilerParams(vmem_limit_bytes=limit * MIB),
        cost_estimate=pl.CostEstimate(
            flops=flops, bytes_accessed=13 * MIB, transcendentals=0
        ),
        name=name,
    )(*args)


def make_power(corpus):
    out = shape(corpus.shape[0] // 128, 128, dtype=F32)
    held = pltpu.VMEM(corpus.shape, BF16)
    return corpus_call(power_kernel, "power", out, [corpus], 2**27, [held])


HALVES = (((0, 0), (0, 1), (0, 3), (1, 0)), ((0, 2), (1, 1), (1, 3), (1, 2)))


def position(chunk):
    a, k, e = chunk
    dp, layer = lax.axis_index("dp"), lax.axis_index("layer")
    x, c = (dp // 2 + 4 - k) % 4, (dp + e) % 2
    block = a if k % 2 == 0 else x // 2
    return (((x % 2) * 2 + c + 4 - layer % 4) % 4) * 2 + block


def place(zh):
    dp, layer = lax.axis_index("dp"), lax.axis_index("layer")
    zl, x, y = dp // 8, dp // 2 % 4, layer % 4
    other = (zh // 2 + zl) % 2
    even = (y // 2 + x) % 2 == 0
    half = jnp.where(even, (zh + x // 2) % 2, other)
    return half, jnp.where(even, other, zh % 2)


def power_rows(power):
    high = power.astype(BF16).astype(F32)
    rest = jnp.zeros((ROWS - 2 * power.shape[0], 128), F32)
    return jnp.concatenate([high, power - high, rest], axis=0).astype(BF16)


def power_of(block, count):
    block = block.astype(F32)
    return block[:count] + block[count : 2 * count]


def dot_block(chunks, pieces, corpus_ref, held, start, step):
    at = pl.ds(start, step)
    rows = jnp.concatenate([piece[...] for piece in pieces], axis=0)
    total = lax.dot_general(
        rows, corpus_ref[at], (((1,), (1,)), ((), ())), preferred_element_type=F32
    ).astype(BF16)
    for j, chunk in enumerate(chunks):
        held[position(chunk), :, at] = total[j * ROWS : (j + 1) * ROWS]


def first_kernel(chunks, *refs):
    count = len(chunks)
    pieces, power_ref, corpus_ref = refs[:count], refs[count], refs[count + 1]
    outs, (corpus, held, sems) = refs[count + 2 : -3], refs[-3:]
    fetch(corpus_ref, corpus, sems, functools.partial(dot_block, chunks, pieces, corpus, held))
    examples = corpus_ref.shape[0]
    power = power_rows(power_ref[...])
    for k in range(4):
        outs[k][:, :, :examples] = held[2 * k : 2 * k + 2]
        outs[k][0, :, examples:] = power
        outs[k][1, :, examples:] = power


def make_first(chunks, pieces, power, corpus):
    examples = corpus.shape[0]
    *totals, held = corpus_call(
        functools.partial(first_kernel, chunks),
        "first",
        [shape(2, ROWS, examples + 128)] * 4 + [shape(examples, WIDTH)],
        [*pieces, power, corpus],
        2 * 256 * examples * WIDTH,
        [pltpu.VMEM((8, ROWS, examples), BF16)],
        30,
    )
    return totals, held


def second_kernel(chunks, *refs):
    count = len(chunks)
    pieces, corpus_ref, outs, held = refs[:count], refs[count], refs[count + 1 : -1], refs[-1]
    for start in range(0, corpus_ref.shape[0], 256):
        dot_block(chunks, pieces, corpus_ref, held, start, 256)
    for k in range(4):
        outs[k][...] = held[2 * k : 2 * k + 2]


def make_second(chunks, pieces, corpus):
    examples = corpus.shape[0]
    return kernel_call(
        functools.partial(second_kernel, chunks),
        "second",
        [shape(2, ROWS, examples)] * 4,
        [*pieces, corpus],
        2 * 256 * examples * WIDTH,
        15 * MIB,
        scratch_shapes=[pltpu.VMEM((8, ROWS, examples), BF16)],
    )


def add_kernel(*refs):
    halves, outs = (refs[:4], refs[4:8]), refs[8:]
    zh = lax.axis_index("layer") // 4
    examples = halves[1][0].shape[2]
    count = examples // 128
    power = power_of(halves[0][0][0, :, examples:], count)
    for k in range(1, 4):
        power = power + power_of(halves[0][k][0, :, examples:], count)
    for m in range(4):
        half, block = place((zh + m) % 4)

        def add(parts):
            total = parts[0][block, :, :examples].astype(F32)
            for k in range(1, 4):
                total = total + parts[k][block, :, :examples].astype(F32)
            outs[m][:, :examples] = total.astype(outs[m].dtype)

        pl.when(half == 0)(functools.partial(add, halves[0]))
        pl.when(half == 1)(functools.partial(add, halves[1]))
        if m == 0:
            outs[m][0:count, examples:] = power
        else:
            outs[m][:, examples:] = power_rows(power)


def add_y(parts):
    examples = parts[4].shape[2]
    outs = [shape(ROWS, examples + 128, dtype=F32 if m == 0 else BF16) for m in range(4)]
    return kernel_call(add_kernel, "add_y", outs, parts, 2**20, 2 * MIB)


def final_kernel(entries, own, a, b, c, out_ref):
    examples = out_ref.shape[2]
    count = examples // 128
    power = own[0:count, examples:]
    for piece in (a, b, c):
        power = power + power_of(piece[:, examples:], count)
    factor = lax.rsqrt(power / entries + 1e-06)
    for j in range(count):
        at = slice(j * 128, (j + 1) * 128)
        total = own[:, at] + a[:, at].astype(F32) + b[:, at].astype(F32) + c[:, at].astype(F32)
        out_ref[:, :, at] = (total * factor[j : j + 1, :]).reshape(16, 2, 128)


def finish(parts, entries):
    examples = parts[0].shape[1] - 128
    return kernel_call(
        functools.partial(final_kernel, entries),
        "finish",
        shape(16, 2, examples, dtype=F32),
        parts,
        2**20,
        MIB,
    )


def per_device(query_grads, corpus_grads, left_inverse, right_inverse):
    corpus = corpus_grads.reshape(corpus_grads.shape[0], WIDTH)
    owned = lax.all_to_all(pack(query_grads[0]), "layer", 0, 0, tiled=True)
    power = make_power(corpus)
    left, right = make_factors(left_inverse[0], right_inverse[0])
    owned, power, left, right = lax.optimization_barrier((owned, power, left, right))
    own = make_ready(owned, left, right)

    other = shifted(own, zl=1)
    pieces = {(0, 0): own, (1, 0): other, (0, 1): shifted(own, x=1), (0, 3): shifted(own, x=3)}
    pieces[0, 2] = shifted(own, x=2)
    pieces[1, 1], pieces[1, 3] = shifted(other, x=1), shifted(other, x=3)
    pieces[1, 2] = shifted(pieces[0, 2], zl=1)

    mine = [pieces[chunk] for chunk in HALVES[0]]
    mine += [shifted(piece, c=1) for piece in mine]
    chunks = [(a, k, e) for e in (0, 1) for a, k in HALVES[0]]
    totals, held = make_first(chunks, mine, power, corpus)

    mine = [pieces[chunk] for chunk in HALVES[1]]
    mine, totals = lax.optimization_barrier((mine, totals))
    parts = [totals[0]] + [shifted(totals[k], y=k) for k in (1, 2, 3)]
    mine += [shifted(piece, c=1) for piece in mine]
    chunks = [(a, k, e) for e in (0, 1) for a, k in HALVES[1]]
    totals = make_second(chunks, mine, held)
    parts += [totals[0]] + [shifted(totals[k], y=k) for k in (1, 2, 3)]
    sums = add_y(parts)
    return finish([sums[0]] + [shifted(sums[m], zh=m) for m in (1, 2, 3)], WIDTH * LAYERS)


def solution(mesh):
    return jax.shard_map(
        per_device,
        mesh=mesh,
        in_specs=(
            P(("dp", "layer"), None, None, None),
            P("dp", "layer", None),
            P("layer", None, None),
            P("layer", None, None),
        ),
        out_specs=P("layer", None, "dp"),
        check_vma=False,
    )
```

```python
import functools

import jax
import jax.numpy as jnp
from jax import lax
from jax.experimental import pallas as pl
from jax.experimental.pallas import tpu as pltpu
from jax.sharding import PartitionSpec as P

F32, BF16 = jnp.float32, jnp.bfloat16
SIZES = {"zl": 2, "x": 4, "c": 2, "zh": 4, "y": 4}
ROWS, WIDTH, LAYERS = 32, 4096, 16
MIB = 1024 * 1024
FETCHES, AHEAD, PARTS = 3, 2, 16
VMEM = pl.BlockSpec(memory_space=pltpu.VMEM)


def kernel_call(body, name, out_shape, args, flops, moved, limit=4, **more):
    single = not isinstance(out_shape, list)
    return pl.pallas_call(
        body,
        in_specs=[VMEM] * len(args),
        out_specs=VMEM if single else [VMEM] * len(out_shape),
        out_shape=out_shape,
        compiler_params=pltpu.CompilerParams(vmem_limit_bytes=limit * MIB),
        cost_estimate=pl.CostEstimate(flops=flops, bytes_accessed=moved, transcendentals=0),
        name=name,
        **more,
    )(*args)


def shape(*sizes, dtype=BF16):
    return jax.ShapeDtypeStruct(sizes, dtype)


def shifted(value, keep=None, **shift):
    pairs = []
    for index in range(256):
        dp, layer = divmod(index, 16)
        at = {"zl": dp // 8, "x": dp // 2 % 4, "c": dp % 2, "zh": layer // 4, "y": layer % 4}
        for name, by in shift.items():
            at[name] = (at[name] + by) % SIZES[name]
        if keep is None or keep(at):
            to = (at["zl"] * 8 + at["x"] * 2 + at["c"]) * 16 + at["zh"] * 4 + at["y"]
            pairs.append((index, to))
    return lax.ppermute(value, ("dp", "layer"), pairs)


def pack_kernel(x_ref, out_ref, scratch):
    for b in range(2):
        for r in range(32):
            piece = x_ref[b, :, r * 128 : (r + 1) * 128].astype(F32)
            scratch[pl.ds(b * 32 + r, LAYERS, stride=64), :] = piece
    out_ref[...] = scratch[...].astype(BF16).reshape(LAYERS, 64, 128)


def pack(x):
    return kernel_call(
        pack_kernel,
        "pack",
        shape(LAYERS, 64, 128),
        [x],
        0,
        2**19,
        scratch_shapes=[pltpu.VMEM((LAYERS * 64, 128), F32)],
    )


def split(value, count):
    pieces = []
    for _ in range(count):
        piece = value.astype(BF16)
        value = value - piece.astype(F32)
        pieces.append(piece)
    return pieces


def product(a, b):
    return jnp.dot(a, b, preferred_element_type=F32)


def factors_kernel(left_ref, right_ref, left_out, right_out):
    row = lax.broadcasted_iota(jnp.int32, (64, 128), 0)
    lane = lax.broadcasted_iota(jnp.int32, (64, 128), 1) % 64
    twice = jnp.where(row == lane, 1.0, 0.0).astype(BF16)
    spread = jnp.where(row == 2 * (lane % 32) + lane // 32, 1.0, 0.0).astype(BF16)
    row = lax.broadcasted_iota(jnp.int32, (64, 64), 0)
    lane = lax.broadcasted_iota(jnp.int32, (64, 64), 1)
    gather = jnp.where(lane == 2 * (row % 32) + row // 32, 1.0, 0.0).astype(BF16)
    zero = jnp.zeros((64, 128), BF16)
    for n, piece in enumerate(split(right_ref[...], 3)):
        double = product(piece, twice).astype(BF16)
        right_out[0:64, n * 256 : n * 256 + 128] = double
        right_out[0:64, n * 256 + 128 : n * 256 + 256] = zero
        right_out[64:128, n * 256 : n * 256 + 128] = zero
        right_out[64:128, n * 256 + 128 : n * 256 + 256] = double
    for n, piece in enumerate(split(left_ref[...], 2)):
        rows = product(gather, piece).astype(BF16)
        left_out[:, n * 128 : (n + 1) * 128] = product(rows, spread).astype(BF16)


def make_factors(left, right):
    return kernel_call(
        factors_kernel,
        "factors",
        [shape(64, 256), shape(128, 768)],
        [left, right],
        2**22,
        2**18,
    )


def ready_kernel(x_ref, left_ref, right_ref, out_ref, scratch):
    x = x_ref[...].reshape(16 * 64, 128)
    y = product(x, right_ref[:, 0:256])
    y = y + product(x, right_ref[:, 256:512])
    y = y + product(x, right_ref[:, 512:768])
    high = y.astype(BF16)
    low = (y - high.astype(F32)).astype(BF16)
    stacks = []
    for i in range(32):
        at = slice(i * 32, (i + 1) * 32)
        column = jnp.concatenate(
            [high[at, :128], high[at, 128:], low[at, :128], low[at, 128:]], axis=0
        )
        stacks.append(jnp.concatenate([column, column], axis=0))
    z = product(left_ref[...], jnp.concatenate(stacks, axis=1))
    first = lax.broadcasted_iota(jnp.int32, (32, 128), 1) < 64
    for i in range(32):
        part = z[:, i * 128 : (i + 1) * 128]
        scratch[i * 32 : (i + 1) * 32, :] = jnp.where(first, part[0:32], part[32:64])
    for r in range(32):
        out_ref[:, r * 128 : (r + 1) * 128] = scratch[pl.ds(r, 32, stride=32), :].astype(BF16)


def make_ready(x, left, right):
    return kernel_call(
        ready_kernel,
        "ready",
        shape(ROWS, WIDTH),
        [x, left, right],
        2**28,
        2**19,
        scratch_shapes=[pltpu.VMEM((1024, 128), F32)],
    )


def fetch(corpus_ref, held_ref, sems, use):
    count = sems.shape[0]
    step = corpus_ref.shape[0] // count

    def copy(start, size, n):
        at = pl.ds(start, size)
        return pltpu.make_async_copy(corpus_ref.at[at], held_ref.at[at], sems.at[n])

    def begin(n):
        for part in range(PARTS):
            copy(n * step + part * step // PARTS, step // PARTS, n).start()

    for n in range(AHEAD):
        begin(n)
    for n in range(count):
        copy(n * step, step, n).wait()
        if n + AHEAD < count:
            begin(n + AHEAD)
        use(n * step, step)


def power_kernel(corpus_ref, out_ref, held_ref, sems):
    def use(start, step):
        totals = []
        for s in range(start, start + step, 32):
            total = None
            for r in range(32):
                piece = held_ref[s : s + 32, r * 128 : (r + 1) * 128].astype(F32)
                total = piece * piece if total is None else total + piece * piece
            totals.append(total)
        power = lax.dot_general(
            jnp.ones((8, 128), F32),
            jnp.concatenate(totals, axis=0),
            (((1,), (1,)), ((), ())),
            precision=lax.Precision.HIGHEST,
            preferred_element_type=F32,
        )[0:1]
        for j in range(step // 128):
            row = start // 128 + j
            out_ref[row : row + 1, :] = power[:, j * 128 : (j + 1) * 128]

    fetch(corpus_ref, held_ref, sems, use)


def corpus_call(body, name, out_shape, args, flops, scratch, limit=50):
    single = not isinstance(out_shape, list)
    return pl.pallas_call(
        body,
        in_specs=[VMEM] * (len(args) - 1) + [pl.BlockSpec(memory_space=pl.ANY)],
        out_specs=VMEM if single else [VMEM] * len(out_shape),
        out_shape=out_shape,
        scratch_shapes=[*scratch, pltpu.SemaphoreType.DMA((FETCHES,))],
        compiler_params=pltpu.CompilerParams(vmem_limit_bytes=limit * MIB),
        cost_estimate=pl.CostEstimate(
            flops=flops, bytes_accessed=13 * MIB, transcendentals=0
        ),
        name=name,
    )(*args)


def make_power(corpus):
    out = shape(corpus.shape[0] // 128, 128, dtype=F32)
    held = pltpu.VMEM(corpus.shape, BF16)
    return corpus_call(power_kernel, "power", out, [corpus], 2**27, [held])


HALVES = (((0, 0), (0, 1), (0, 3), (1, 0)), ((0, 2), (1, 1), (1, 3), (1, 2)))


def position(chunk):
    a, k, e = chunk
    dp, layer = lax.axis_index("dp"), lax.axis_index("layer")
    x, c = (dp // 2 + 4 - k) % 4, (dp + e) % 2
    block = a if k % 2 == 0 else x // 2
    return (((x % 2) * 2 + c + 4 - layer % 4) % 4) * 2 + block


def place(zh):
    dp, layer = lax.axis_index("dp"), lax.axis_index("layer")
    zl, x, y = dp // 8, dp // 2 % 4, layer % 4
    other = (zh // 2 + zl) % 2
    even = (y // 2 + x) % 2 == 0
    half = jnp.where(even, (zh + x // 2) % 2, other)
    return half, jnp.where(even, other, zh % 2)


def power_rows(power):
    high = power.astype(BF16).astype(F32)
    rest = jnp.zeros((ROWS - 2 * power.shape[0], 128), F32)
    return jnp.concatenate([high, power - high, rest], axis=0).astype(BF16)


def power_of(block, count):
    block = block.astype(F32)
    return block[:count] + block[count : 2 * count]


def dot_block(chunks, pieces, corpus_ref, held, start, step):
    at = pl.ds(start, step)
    rows = jnp.concatenate([piece[...] for piece in pieces], axis=0)
    total = lax.dot_general(
        rows, corpus_ref[at], (((1,), (1,)), ((), ())), preferred_element_type=F32
    ).astype(BF16)
    for j, chunk in enumerate(chunks):
        held[position(chunk), :, at] = total[j * ROWS : (j + 1) * ROWS]


def first_kernel(chunks, *refs):
    count = len(chunks)
    pieces, power_ref, corpus_ref = refs[:count], refs[count], refs[count + 1]
    outs, (corpus, held, sems) = refs[count + 2 : -3], refs[-3:]
    fetch(corpus_ref, corpus, sems, functools.partial(dot_block, chunks, pieces, corpus, held))
    examples = corpus_ref.shape[0]
    power = power_rows(power_ref[...])
    for k in range(4):
        outs[k][:, :, :examples] = held[2 * k : 2 * k + 2]
        outs[k][0, :, examples:] = power
        outs[k][1, :, examples:] = power


def make_first(chunks, pieces, power, corpus):
    examples = corpus.shape[0]
    *totals, held = corpus_call(
        functools.partial(first_kernel, chunks),
        "first",
        [shape(2, ROWS, examples + 128)] * 4 + [shape(examples, WIDTH)],
        [*pieces, power, corpus],
        2 * 256 * examples * WIDTH,
        [pltpu.VMEM((8, ROWS, examples), BF16)],
        30,
    )
    return totals, held


def second_kernel(chunks, *refs):
    count = len(chunks)
    pieces, corpus_ref, outs, held = refs[:count], refs[count], refs[count + 1 : -1], refs[-1]
    for start in range(0, corpus_ref.shape[0], 256):
        dot_block(chunks, pieces, corpus_ref, held, start, 256)
    for k in range(4):
        outs[k][...] = held[2 * k : 2 * k + 2]


def make_second(chunks, pieces, corpus):
    examples = corpus.shape[0]
    return kernel_call(
        functools.partial(second_kernel, chunks),
        "second",
        [shape(2, ROWS, examples)] * 4,
        [*pieces, corpus],
        2 * 256 * examples * WIDTH,
        15 * MIB,
        scratch_shapes=[pltpu.VMEM((8, ROWS, examples), BF16)],
    )


def add_kernel(*refs):
    halves, outs = (refs[:4], refs[4:8]), refs[8:]
    zh = lax.axis_index("layer") // 4
    examples = halves[1][0].shape[2]
    count = examples // 128
    power = power_of(halves[0][0][0, :, examples:], count)
    for k in range(1, 4):
        power = power + power_of(halves[0][k][0, :, examples:], count)
    for m in range(4):
        half, block = place((zh + m) % 4)

        def add(parts):
            total = parts[0][block, :, :examples].astype(F32)
            for k in range(1, 4):
                total = total + parts[k][block, :, :examples].astype(F32)
            outs[m][:, :examples] = total.astype(outs[m].dtype)

        pl.when(half == 0)(functools.partial(add, halves[0]))
        pl.when(half == 1)(functools.partial(add, halves[1]))
        if m == 0:
            outs[m][0:count, examples:] = power
        else:
            outs[m][:, examples:] = power_rows(power)


def add_y(parts):
    examples = parts[4].shape[2]
    outs = [shape(ROWS, examples + 128, dtype=F32 if m == 0 else BF16) for m in range(4)]
    return kernel_call(add_kernel, "add_y", outs, parts, 2**20, 2 * MIB)


def final_kernel(entries, own, a, b, c, out_ref):
    examples = out_ref.shape[2]
    count = examples // 128
    power = own[0:count, examples:]
    for piece in (a, b, c):
        power = power + power_of(piece[:, examples:], count)
    factor = lax.rsqrt(power / entries + 1e-06)
    for j in range(count):
        at = slice(j * 128, (j + 1) * 128)
        total = own[:, at] + a[:, at].astype(F32) + b[:, at].astype(F32) + c[:, at].astype(F32)
        out_ref[:, :, at] = (total * factor[j : j + 1, :]).reshape(16, 2, 128)


def finish(parts, entries):
    examples = parts[0].shape[1] - 128
    return kernel_call(
        functools.partial(final_kernel, entries),
        "finish",
        shape(16, 2, examples, dtype=F32),
        parts,
        2**20,
        MIB,
    )


def per_device(query_grads, corpus_grads, left_inverse, right_inverse):
    corpus = corpus_grads.reshape(corpus_grads.shape[0], WIDTH)
    owned = lax.all_to_all(pack(query_grads[0]), "layer", 0, 0, tiled=True)
    power = make_power(corpus)
    left, right = make_factors(left_inverse[0], right_inverse[0])
    owned, power, left, right = lax.optimization_barrier((owned, power, left, right))
    own = make_ready(owned, left, right)

    other = shifted(own, zl=1)
    pieces = {(0, 0): own, (1, 0): other, (0, 1): shifted(own, x=1), (0, 3): shifted(own, x=3)}
    pieces[0, 2] = shifted(own, x=2)
    pieces[1, 1], pieces[1, 3] = shifted(other, x=1), shifted(other, x=3)

    arrived = (pieces[0, 1], pieces[0, 3], pieces[0, 2])
    pieces[0, 1], pieces[0, 3], pieces[0, 2] = lax.optimization_barrier(arrived)
    pieces[1, 2] = shifted(pieces[0, 2], zl=1)
    mine = [pieces[chunk] for chunk in HALVES[0]]
    mine += [shifted(piece, c=1) for piece in mine]
    chunks = [(a, k, e) for e in (0, 1) for a, k in HALVES[0]]
    totals, held = make_first(chunks, mine, power, corpus)

    mine = [pieces[chunk] for chunk in HALVES[1]]
    mine, totals = lax.optimization_barrier((mine, totals))
    parts = [totals[0]] + [shifted(totals[k], y=k) for k in (1, 2, 3)]
    mine += [shifted(piece, c=1) for piece in mine]
    chunks = [(a, k, e) for e in (0, 1) for a, k in HALVES[1]]
    totals = make_second(chunks, mine, held)
    parts += [totals[0]] + [shifted(totals[k], y=k) for k in (1, 2, 3)]
    sums = add_y(parts)
    return finish([sums[0]] + [shifted(sums[m], zh=m) for m in (1, 2, 3)], WIDTH * LAYERS)


def solution(mesh):
    return jax.shard_map(
        per_device,
        mesh=mesh,
        in_specs=(
            P(("dp", "layer"), None, None, None),
            P("dp", "layer", None),
            P("layer", None, None),
            P("layer", None, None),
        ),
        out_specs=P("layer", None, "dp"),
        check_vma=False,
    )
```

```python
import functools

import jax
import jax.numpy as jnp
from jax import lax
from jax.experimental import pallas as pl
from jax.experimental.pallas import tpu as pltpu
from jax.sharding import PartitionSpec as P

F32, BF16 = jnp.float32, jnp.bfloat16
SIZES = {"zl": 2, "x": 4, "c": 2, "zh": 4, "y": 4}
ROWS, WIDTH, LAYERS = 32, 4096, 16
MIB = 1024 * 1024
FETCHES, AHEAD, PARTS = 3, 2, 16
VMEM = pl.BlockSpec(memory_space=pltpu.VMEM)


def kernel_call(body, name, out_shape, args, flops, moved, limit=4, **more):
    single = not isinstance(out_shape, list)
    return pl.pallas_call(
        body,
        in_specs=[VMEM] * len(args),
        out_specs=VMEM if single else [VMEM] * len(out_shape),
        out_shape=out_shape,
        compiler_params=pltpu.CompilerParams(vmem_limit_bytes=limit * MIB),
        cost_estimate=pl.CostEstimate(flops=flops, bytes_accessed=moved, transcendentals=0),
        name=name,
        **more,
    )(*args)


def shape(*sizes, dtype=BF16):
    return jax.ShapeDtypeStruct(sizes, dtype)


def shifted(value, keep=None, **shift):
    pairs = []
    for index in range(256):
        dp, layer = divmod(index, 16)
        at = {"zl": dp // 8, "x": dp // 2 % 4, "c": dp % 2, "zh": layer // 4, "y": layer % 4}
        for name, by in shift.items():
            at[name] = (at[name] + by) % SIZES[name]
        if keep is None or keep(at):
            to = (at["zl"] * 8 + at["x"] * 2 + at["c"]) * 16 + at["zh"] * 4 + at["y"]
            pairs.append((index, to))
    return lax.ppermute(value, ("dp", "layer"), pairs)


def pack_kernel(x_ref, out_ref, scratch):
    for r in range(32):
        piece = x_ref[0, :, r * 128 : (r + 1) * 128].astype(F32)
        scratch[pl.ds(r, LAYERS, stride=32), :] = piece
    out_ref[...] = scratch[...].astype(BF16).reshape(LAYERS, 32, 128)


def pack(x):
    return pl.pallas_call(
        pack_kernel,
        grid=(2,),
        in_specs=[pl.BlockSpec((1, LAYERS, WIDTH), lambda b: (b, 0, 0))],
        out_specs=pl.BlockSpec((LAYERS, 32, 128), lambda b: (0, b, 0)),
        out_shape=shape(LAYERS, 64, 128),
        scratch_shapes=[pltpu.VMEM((LAYERS * 32, 128), F32)],
        compiler_params=pltpu.CompilerParams(vmem_limit_bytes=56 * MIB),
        cost_estimate=pl.CostEstimate(flops=0, bytes_accessed=2**19, transcendentals=0),
        name="pack",
    )(x)


def split(value, count):
    pieces = []
    for _ in range(count):
        piece = value.astype(BF16)
        value = value - piece.astype(F32)
        pieces.append(piece)
    return pieces


def product(a, b):
    return jnp.dot(a, b, preferred_element_type=F32)


def factors_kernel(left_ref, right_ref, left_out, right_out):
    row = lax.broadcasted_iota(jnp.int32, (64, 128), 0)
    lane = lax.broadcasted_iota(jnp.int32, (64, 128), 1) % 64
    twice = jnp.where(row == lane, 1.0, 0.0).astype(BF16)
    spread = jnp.where(row == 2 * (lane % 32) + lane // 32, 1.0, 0.0).astype(BF16)
    row = lax.broadcasted_iota(jnp.int32, (64, 64), 0)
    lane = lax.broadcasted_iota(jnp.int32, (64, 64), 1)
    gather = jnp.where(lane == 2 * (row % 32) + row // 32, 1.0, 0.0).astype(BF16)
    zero = jnp.zeros((64, 128), BF16)
    for n, piece in enumerate(split(right_ref[...], 3)):
        double = product(piece, twice).astype(BF16)
        right_out[0:64, n * 256 : n * 256 + 128] = double
        right_out[0:64, n * 256 + 128 : n * 256 + 256] = zero
        right_out[64:128, n * 256 : n * 256 + 128] = zero
        right_out[64:128, n * 256 + 128 : n * 256 + 256] = double
    for n, piece in enumerate(split(left_ref[...], 2)):
        rows = product(gather, piece).astype(BF16)
        left_out[:, n * 128 : (n + 1) * 128] = product(rows, spread).astype(BF16)


def make_factors(left, right):
    return kernel_call(
        factors_kernel,
        "factors",
        [shape(64, 256), shape(128, 768)],
        [left, right],
        2**22,
        2**18,
    )


def ready_kernel(x_ref, left_ref, right_ref, out_ref, scratch):
    x = x_ref[...].reshape(16 * 64, 128)
    y = product(x, right_ref[:, 0:256])
    y = y + product(x, right_ref[:, 256:512])
    y = y + product(x, right_ref[:, 512:768])
    high = y.astype(BF16)
    low = (y - high.astype(F32)).astype(BF16)
    stacks = []
    for i in range(32):
        at = slice(i * 32, (i + 1) * 32)
        column = jnp.concatenate(
            [high[at, :128], high[at, 128:], low[at, :128], low[at, 128:]], axis=0
        )
        stacks.append(jnp.concatenate([column, column], axis=0))
    z = product(left_ref[...], jnp.concatenate(stacks, axis=1))
    first = lax.broadcasted_iota(jnp.int32, (32, 128), 1) < 64
    for i in range(32):
        part = z[:, i * 128 : (i + 1) * 128]
        scratch[i * 32 : (i + 1) * 32, :] = jnp.where(first, part[0:32], part[32:64])
    for r in range(32):
        out_ref[:, r * 128 : (r + 1) * 128] = scratch[pl.ds(r, 32, stride=32), :].astype(BF16)


def make_ready(x, left, right):
    return kernel_call(
        ready_kernel,
        "ready",
        shape(ROWS, WIDTH),
        [x, left, right],
        2**28,
        2**19,
        scratch_shapes=[pltpu.VMEM((1024, 128), F32)],
    )


def fetch(corpus_ref, held_ref, sems, use):
    count = sems.shape[0]
    step = corpus_ref.shape[0] // count

    def copy(start, size, n):
        at = pl.ds(start, size)
        return pltpu.make_async_copy(corpus_ref.at[at], held_ref.at[at], sems.at[n])

    def begin(n):
        for part in range(PARTS):
            copy(n * step + part * step // PARTS, step // PARTS, n).start()

    for n in range(AHEAD):
        begin(n)
    for n in range(count):
        copy(n * step, step, n).wait()
        if n + AHEAD < count:
            begin(n + AHEAD)
        use(n * step, step)


def power_kernel(corpus_ref, out_ref, held_ref, sems):
    def use(start, step):
        totals = []
        for s in range(start, start + step, 32):
            total = None
            for r in range(32):
                piece = held_ref[s : s + 32, r * 128 : (r + 1) * 128].astype(F32)
                total = piece * piece if total is None else total + piece * piece
            totals.append(total)
        power = lax.dot_general(
            jnp.ones((8, 128), F32),
            jnp.concatenate(totals, axis=0),
            (((1,), (1,)), ((), ())),
            precision=lax.Precision.HIGHEST,
            preferred_element_type=F32,
        )[0:1]
        for j in range(step // 128):
            row = start // 128 + j
            out_ref[row : row + 1, :] = power[:, j * 128 : (j + 1) * 128]

    fetch(corpus_ref, held_ref, sems, use)


def corpus_call(body, name, out_shape, args, flops, scratch, limit=50):
    single = not isinstance(out_shape, list)
    return pl.pallas_call(
        body,
        in_specs=[VMEM] * (len(args) - 1) + [pl.BlockSpec(memory_space=pl.ANY)],
        out_specs=VMEM if single else [VMEM] * len(out_shape),
        out_shape=out_shape,
        scratch_shapes=[*scratch, pltpu.SemaphoreType.DMA((FETCHES,))],
        compiler_params=pltpu.CompilerParams(vmem_limit_bytes=limit * MIB),
        cost_estimate=pl.CostEstimate(
            flops=flops, bytes_accessed=13 * MIB, transcendentals=0
        ),
        name=name,
    )(*args)


def make_power(corpus):
    out = shape(corpus.shape[0] // 128, 128, dtype=F32)
    held = pltpu.VMEM(corpus.shape, BF16)
    return corpus_call(power_kernel, "power", out, [corpus], 2**27, [held])


HALVES = (((0, 0), (0, 1), (0, 3), (1, 0)), ((0, 2), (1, 1), (1, 3), (1, 2)))


def position(chunk):
    a, k, e = chunk
    dp, layer = lax.axis_index("dp"), lax.axis_index("layer")
    x, c = (dp // 2 + 4 - k) % 4, (dp + e) % 2
    block = a if k % 2 == 0 else x // 2
    return (((x % 2) * 2 + c + 4 - layer % 4) % 4) * 2 + block


def place(zh):
    dp, layer = lax.axis_index("dp"), lax.axis_index("layer")
    zl, x, y = dp // 8, dp // 2 % 4, layer % 4
    other = (zh // 2 + zl) % 2
    even = (y // 2 + x) % 2 == 0
    half = jnp.where(even, (zh + x // 2) % 2, other)
    return half, jnp.where(even, other, zh % 2)


def power_rows(power):
    high = power.astype(BF16).astype(F32)
    rest = jnp.zeros((ROWS - 2 * power.shape[0], 128), F32)
    return jnp.concatenate([high, power - high, rest], axis=0).astype(BF16)


def power_of(block, count):
    block = block.astype(F32)
    return block[:count] + block[count : 2 * count]


def dot_block(chunks, pieces, corpus_ref, held, start, step):
    at = pl.ds(start, step)
    rows = jnp.concatenate([piece[...] for piece in pieces], axis=0)
    total = lax.dot_general(
        rows, corpus_ref[at], (((1,), (1,)), ((), ())), preferred_element_type=F32
    ).astype(BF16)
    for j, chunk in enumerate(chunks):
        held[position(chunk), :, at] = total[j * ROWS : (j + 1) * ROWS]


def first_kernel(chunks, *refs):
    count = len(chunks)
    pieces, power_ref, corpus_ref = refs[:count], refs[count], refs[count + 1]
    outs, (corpus, held, sems) = refs[count + 2 : -3], refs[-3:]
    fetch(corpus_ref, corpus, sems, functools.partial(dot_block, chunks, pieces, corpus, held))
    examples = corpus_ref.shape[0]
    power = power_rows(power_ref[...])
    for k in range(4):
        outs[k][:, :, :examples] = held[2 * k : 2 * k + 2]
        outs[k][0, :, examples:] = power
        outs[k][1, :, examples:] = power


def make_first(chunks, pieces, power, corpus):
    examples = corpus.shape[0]
    *totals, held = corpus_call(
        functools.partial(first_kernel, chunks),
        "first",
        [shape(2, ROWS, examples + 128)] * 4 + [shape(examples, WIDTH)],
        [*pieces, power, corpus],
        2 * 256 * examples * WIDTH,
        [pltpu.VMEM((8, ROWS, examples), BF16)],
        30,
    )
    return totals, held


def second_kernel(chunks, *refs):
    count = len(chunks)
    pieces, corpus_ref, outs, held = refs[:count], refs[count], refs[count + 1 : -1], refs[-1]
    for start in range(0, corpus_ref.shape[0], 256):
        dot_block(chunks, pieces, corpus_ref, held, start, 256)
    for k in range(4):
        outs[k][...] = held[2 * k : 2 * k + 2]


def make_second(chunks, pieces, corpus):
    examples = corpus.shape[0]
    return kernel_call(
        functools.partial(second_kernel, chunks),
        "second",
        [shape(2, ROWS, examples)] * 4,
        [*pieces, corpus],
        2 * 256 * examples * WIDTH,
        15 * MIB,
        scratch_shapes=[pltpu.VMEM((8, ROWS, examples), BF16)],
    )


def add_kernel(*refs):
    halves, outs = (refs[:4], refs[4:8]), refs[8:]
    zh = lax.axis_index("layer") // 4
    examples = halves[1][0].shape[2]
    count = examples // 128
    power = power_of(halves[0][0][0, :, examples:], count)
    for k in range(1, 4):
        power = power + power_of(halves[0][k][0, :, examples:], count)
    for m in range(4):
        half, block = place((zh + m) % 4)

        def add(parts):
            total = parts[0][block, :, :examples].astype(F32)
            for k in range(1, 4):
                total = total + parts[k][block, :, :examples].astype(F32)
            outs[m][:, :examples] = total.astype(outs[m].dtype)

        pl.when(half == 0)(functools.partial(add, halves[0]))
        pl.when(half == 1)(functools.partial(add, halves[1]))
        if m == 0:
            outs[m][0:count, examples:] = power
        else:
            outs[m][:, examples:] = power_rows(power)


def add_y(parts):
    examples = parts[4].shape[2]
    outs = [shape(ROWS, examples + 128, dtype=F32 if m == 0 else BF16) for m in range(4)]
    return kernel_call(add_kernel, "add_y", outs, parts, 2**20, 2 * MIB)


def final_kernel(entries, own, a, b, c, out_ref):
    examples = out_ref.shape[2]
    count = examples // 128
    power = own[0:count, examples:]
    for piece in (a, b, c):
        power = power + power_of(piece[:, examples:], count)
    factor = lax.rsqrt(power / entries + 1e-06)
    for j in range(count):
        at = slice(j * 128, (j + 1) * 128)
        total = own[:, at] + a[:, at].astype(F32) + b[:, at].astype(F32) + c[:, at].astype(F32)
        out_ref[:, :, at] = (total * factor[j : j + 1, :]).reshape(16, 2, 128)


def finish(parts, entries):
    examples = parts[0].shape[1] - 128
    return kernel_call(
        functools.partial(final_kernel, entries),
        "finish",
        shape(16, 2, examples, dtype=F32),
        parts,
        2**20,
        MIB,
    )


def per_device(query_grads, corpus_grads, left_inverse, right_inverse):
    corpus = corpus_grads.reshape(corpus_grads.shape[0], WIDTH)
    owned = lax.all_to_all(pack(query_grads[0]), "layer", 0, 0, tiled=True)
    power = make_power(corpus)
    left, right = make_factors(left_inverse[0], right_inverse[0])
    owned, power, left, right = lax.optimization_barrier((owned, power, left, right))
    own = make_ready(owned, left, right)

    other = shifted(own, zl=1)
    pieces = {(0, 0): own, (1, 0): other, (0, 1): shifted(own, x=1), (0, 3): shifted(own, x=3)}
    pieces[0, 2] = shifted(own, x=2)
    pieces[1, 1], pieces[1, 3] = shifted(other, x=1), shifted(other, x=3)

    arrived = (pieces[0, 1], pieces[0, 3], pieces[0, 2])
    pieces[0, 1], pieces[0, 3], pieces[0, 2] = lax.optimization_barrier(arrived)
    pieces[1, 2] = shifted(pieces[0, 2], zl=1)
    mine = [pieces[chunk] for chunk in HALVES[0]]
    mine += [shifted(piece, c=1) for piece in mine]
    chunks = [(a, k, e) for e in (0, 1) for a, k in HALVES[0]]
    totals, held = make_first(chunks, mine, power, corpus)

    mine = [pieces[chunk] for chunk in HALVES[1]]
    mine, totals = lax.optimization_barrier((mine, totals))
    parts = [totals[0]] + [shifted(totals[k], y=k) for k in (1, 2, 3)]
    mine += [shifted(piece, c=1) for piece in mine]
    chunks = [(a, k, e) for e in (0, 1) for a, k in HALVES[1]]
    totals = make_second(chunks, mine, held)
    parts += [totals[0]] + [shifted(totals[k], y=k) for k in (1, 2, 3)]
    sums = add_y(parts)
    return finish([sums[0]] + [shifted(sums[m], zh=m) for m in (1, 2, 3)], WIDTH * LAYERS)


def solution(mesh):
    return jax.shard_map(
        per_device,
        mesh=mesh,
        in_specs=(
            P(("dp", "layer"), None, None, None),
            P("dp", "layer", None),
            P("layer", None, None),
            P("layer", None, None),
        ),
        out_specs=P("layer", None, "dp"),
        check_vma=False,
    )
```
